512 devices in a mesh: lvl: 16 (over z, core), fib: 32 (over y, x).
Axes of the slice: x: 4, y: 8, z: 8, core: 2. Of those that a mesh axis runs over, the one named last changes fastest.
Arguments:
- coefficients: float32 [256, 512, 1024], P('lvl', 'fib'), may hold values from -6 to 6
- local_vol: float32 [256, 512], P('lvl', 'fib'), may hold values from 0.1 to 0.6
Outputs:
- result: float32 [256, 512, 1024], P('lvl', 'fib')
The draws below stay inside these ranges and needn't reach their ends.
All inputs are finite; a program needn't handle non-finite values.
Results may differ from the reference program's by a relative error of at most 0.00013.
Values sent between devices are 32-bit elements; how exact they have to be, the bound alone decides.
No kernel may reach another device: no remote copies, remote signals or barrier semaphores. Data moves between devices by JAX's collectives and lax.ppermute only.
A program may use at most 64 MiB of HBM per device.

```python
import math
import jax
import jax.numpy as jnp

COLS = 1024
NA = 512
NB = 256


def steps_of(stream_key, dims, shards, least, top_value):
    loudness = 1.0
    for axis_at, shards_of in shards:
        heights = jax.random.uniform(jax.random.fold_in(jax.random.fold_in(stream_key, 6), axis_at), (shards_of,), jnp.float32, least / len(shards), top_value / len(shards))
        loudness = loudness * jnp.repeat(jnp.exp(heights), dims[axis_at] // shards_of).reshape((-1,) + (1,) * (len(dims) - 1 - axis_at))
    return loudness


def centred(key, shape, scale, limit, pieces=(), kind=jnp.bfloat16):
    values = jax.random.normal(key, shape, jnp.float32) * scale
    if len(pieces) > 0:
        values = steps_of(key, shape, pieces, -0.22, 0.18) * values
    return jnp.clip(values, min=-limit, max=limit).astype(kind)


def setup_inputs(seed: int = 0) -> dict:
    seeds = jax.random.split(jax.random.key(seed), 3)
    coefficients = centred(seeds[0], (NB, NA, COLS), 1.0, 6.0, ((0, 16), (1, 32)), jnp.float32)
    local_vol = jnp.clip(jnp.exp(math.log(0.6) - 1.7917595 * jax.random.uniform(seeds[1], (NB, NA), jnp.float32) ** steps_of(seeds[1], (NB, NA), ((0, 16), (1, 32)), -0.2, 0.2)), 0.1, 0.6)
    return {"coefficients": coefficients, "local_vol": local_vol}


KAPPA_SCALE = 8.0
DRIFT = 0.2
DISCOUNT = 0.05


def half_widths(count):
    index = jnp.arange(count, dtype=jnp.int32)
    lowest = index & (-index)
    return jnp.where(index == 0, count, lowest).astype(jnp.float32)


def descend(values):
    count = values.shape[0]
    step = count // 2
    while step >= 1:
        padded = jnp.concatenate([values, jnp.zeros_like(values[:1])], axis=0)
        ends = padded[0::2 * step]
        middle = values[step::2 * step] + 0.5 * (ends[:-1] + ends[1:])
        values = values.at[step::2 * step].set(middle)
        step = step // 2
    return values


def ascend(values):
    count = values.shape[0]
    step = 1
    while step < count:
        half = 0.5 * values[step::2 * step]
        values = values.at[0::2 * step].add(half)
        values = values.at[2 * step::2 * step].add(half[:-1])
        step = step * 2
    return values


def stencil(nodal, sigma, place):
    kappa = KAPPA_SCALE * 0.5 * sigma * sigma * place * place
    beta = DRIFT * place
    zero_row = jnp.zeros_like(nodal[:1])
    below = jnp.concatenate([zero_row, nodal[:-1]], axis=0)
    above = jnp.concatenate([nodal[1:], zero_row], axis=0)
    return (2.0 / 3.0 + 2.0 * kappa + DISCOUNT) * nodal + (1.0 / 6.0 - kappa + beta) * below + (1.0 / 6.0 - kappa - beta) * above


def one_pass(values, sigma):
    count = values.shape[0]
    place = (jnp.arange(count, dtype=jnp.float32) / count)[:, None, None]
    nodal = descend(values)
    image = stencil(nodal, sigma, place)
    return ascend(image) / half_widths(count)[:, None, None]


def reference(coefficients, local_vol):
    along_a = jnp.transpose(coefficients, (1, 0, 2))
    sigma_a = jnp.transpose(local_vol)[:, :, None]
    after_a = jnp.transpose(one_pass(along_a, sigma_a), (1, 0, 2))
    return one_pass(after_a, local_vol[:, :, None])
```

```python
import functools

import jax
import jax.numpy as jnp
from jax import lax
from jax.experimental import pallas as pl
from jax.experimental.pallas import tpu as pltpu
from jax.sharding import PartitionSpec as P

KAPPA_SCALE = 8.0
DRIFT = 0.2
DISCOUNT = 0.05
CENTRE = 2.0 / 3.0 + DISCOUNT
SIDE = 1.0 / 6.0
LINEAR = CENTRE + 2.0 * SIDE
LANES = 128
VMEM_LIMIT = 32 * 1024 * 1024


def descend(rows, low, high):
    n = len(rows)
    nodal = [low] + [None] * (n - 1) + [high]
    step = n // 2
    while step >= 1:
        for at in range(step, n, 2 * step):
            left, right = nodal[at - step], nodal[at + step]
            if left is None and right is None:
                nodal[at] = rows[at]
            elif left is None or right is None:
                nodal[at] = rows[at] + 0.5 * (right if left is None else left)
            else:
                nodal[at] = rows[at] + 0.5 * (left + right)
        step //= 2
    return nodal


def add(a, b):
    if a is None:
        return b
    return a if b is None else a + b


def ascend(rows):
    n = len(rows)
    sums = list(rows) + [None]
    step = 1
    while step < n:
        for at in range(step, n, 2 * step):
            half = 0.5 * sums[at]
            sums[at - step] = add(sums[at - step], half)
            sums[at + step] = add(sums[at + step], half)
        step *= 2
    return sums


def lowest(index):
    return index & -index


def local_pass(rows, kappas, first_beta, total):
    n = len(rows)
    nodal = descend(rows, None, None)
    images = []
    for at in range(n):
        beta = first_beta + DRIFT * at / total
        kappa = kappas(at)
        above = nodal[at + 1]
        if at == 0:
            images.append((SIDE - beta - kappa) * above)
            continue
        below = nodal[at - 1]
        middle = nodal[at]
        image = (CENTRE + 2.0 * kappa) * middle
        if below is not None:
            image = image + (SIDE + beta - kappa) * below
        if above is not None:
            image = image + (SIDE - beta - kappa) * above
        images.append(image)
    sums = ascend(images)
    fine = [sums[at] * (1.0 / lowest(at)) for at in range(1, n)]
    return fine, (rows[0], sums[0], sums[n], nodal[n - 1])


def end_weights(at, n, first_beta, total):
    tilt = (first_beta + DRIFT * at / total) * (2.0 / n)
    return LINEAR * (1.0 - at / n) + tilt, LINEAR * (at / n) - tilt


def coarse_pass(heads, lefts, rights, lasts, kappas, n):
    count = len(heads)
    total = n * count
    inner = descend([None] + heads[1:], heads[0], None)
    node = inner[:count]
    share = [r / n for r in range(n)]
    left0 = sum(1 - s for s in share[1:])
    left1 = sum((1 - s) ** 2 for s in share[1:])
    left2 = sum((1 - s) * s for s in share[1:])
    left3 = sum((1 - s) * s * n for s in share[1:])
    right0 = sum(share[1:])
    right1 = left2
    right2 = sum(s * s for s in share[1:])
    right3 = sum(s * s * n for s in share[1:])
    slope = DRIFT / total
    duals = []
    for i in range(count):
        beta = DRIFT * i / count
        kappa = kappas[i]
        tilt = (2.0 / n) * (beta * left0 + slope * left3)
        following = node[i + 1] if i + 1 < count else None
        upper = SIDE - beta - kappa
        own = CENTRE + 2.0 * kappa + upper * (1.0 - 1.0 / n) + (LINEAR * left1 + tilt)
        dual = lefts[i]
        if following is not None:
            dual = dual + (upper * (1.0 / n) + (LINEAR * left2 - tilt)) * following
        if i > 0:
            before_beta = DRIFT * (i - 1) / count
            tilt = (2.0 / n) * (before_beta * right0 + slope * right3)
            lower = SIDE + beta - kappa
            own = own + lower * (1.0 - 1.0 / n) + (LINEAR * right2 - tilt)
            dual = dual + rights[i - 1] + lower * lasts[i - 1]
            dual = dual + (lower * (1.0 / n) + (LINEAR * right1 + tilt)) * node[i - 1]
        duals.append(dual + own * node[i])
    sums = ascend(duals)
    outs = [sums[i] * (1.0 / (total if i == 0 else n * lowest(i))) for i in range(count)]
    return node, outs


def first_kernel(count, values_ref, vol_ref, packet_ref, fine_ref, kappa_ref):
    nb, n, cols = values_ref.shape
    tiles = cols // LANES
    total = n * count
    index = lax.axis_index("fib").astype(jnp.float32)
    first_beta = index * (DRIFT / count)
    vol = vol_ref[...]
    for r in range(n):
        place = index * (1.0 / count) + r / total
        root = vol[:, r : r + 1] * place
        kappa_ref[r] = jnp.broadcast_to((KAPPA_SCALE * 0.5) * root * root, (nb, LANES))
    parts = count // nb
    per = tiles // parts
    rows = 4 * per + 1
    stride = parts * rows
    for part in range(parts):
        packet_ref[pl.ds(part * rows + rows - 1, nb, stride=stride), :] = kappa_ref[0]
    for t in range(tiles):
        lanes = slice(t * LANES, (t + 1) * LANES)
        block = jnp.swapaxes(values_ref[:, :, lanes], 0, 1)
        fine, quads = local_pass([block[r] for r in range(n)], lambda r: kappa_ref[r], first_beta, total)
        zero = jnp.zeros_like(fine[0])
        fine_ref[:, :, lanes] = jnp.swapaxes(jnp.stack([zero] + fine), 0, 1)
        for q, quad in enumerate(quads):
            start = (t // per) * rows + q * per + t % per
            packet_ref[pl.ds(start, nb, stride=stride), :] = quad


def coarse_kernel(count, n, per, packet_ref, answer_ref):
    rows = 4 * per + 1

    def piece(i, q):
        return packet_ref[i * rows + q * per : i * rows + (q + 1) * per, :]

    quads = [[piece(i, q) for i in range(count)] for q in range(4)]
    kappas = [packet_ref[(i + 1) * rows - 1 : (i + 1) * rows, :] for i in range(count)]
    node, outs = coarse_pass(*quads, kappas, n)
    for i in range(count):
        base = 3 * per * i
        answer_ref[base : base + per, :] = node[i]
        answer_ref[base + per : base + 2 * per, :] = (
            node[i + 1] if i + 1 < count else jnp.zeros_like(node[i])
        )
        answer_ref[base + 2 * per : base + 3 * per, :] = outs[i]


def second_kernel(fib_count, lvl_count, answer_ref, fine_ref, vol_ref, packet_ref, next_ref, kappa_ref):
    n, na, cols = fine_ref.shape
    tiles = cols // LANES
    fib_total = na * fib_count
    total = n * lvl_count
    fib_beta = lax.axis_index("fib").astype(jnp.float32) * (DRIFT / fib_count)
    index = lax.axis_index("lvl").astype(jnp.float32)
    first_beta = index * (DRIFT / lvl_count)
    vol = vol_ref[...]
    diagonal = lax.broadcasted_iota(jnp.int32, (na, na), 0) == lax.broadcasted_iota(
        jnp.int32, (na, na), 1
    )
    for r in range(n):
        place = index * (1.0 / lvl_count) + r / total
        column = jnp.sum(jnp.where(diagonal, vol[r : r + 1, :], 0.0), axis=1, keepdims=True)
        root = column * place
        kappa_ref[r] = jnp.broadcast_to((KAPPA_SCALE * 0.5) * root * root, (na, LANES))
    at = lax.broadcasted_iota(jnp.int32, (na, LANES), 0)
    tilt = (fib_beta + at.astype(jnp.float32) * (DRIFT / fib_total)) * (2.0 / na)
    share = at.astype(jnp.float32) * (1.0 / na)
    is_head = at == 0
    low = LINEAR * (1.0 - share) + tilt
    high = LINEAR * share - tilt
    parts = fib_count // n
    per = tiles // parts
    rows = 4 * tiles + 1
    packet_ref[pl.ds(rows - 1, na, stride=rows), :] = kappa_ref[0]
    for t in range(tiles):
        lanes = slice(t * LANES, (t + 1) * LANES)
        block = []
        for b in range(n):
            base = (b * parts + t // per) * 3 * per + t % per
            own = answer_ref[base : base + 1, :]
            following = answer_ref[base + per : base + per + 1, :]
            head = answer_ref[base + 2 * per : base + 2 * per + 1, :]
            body = fine_ref[b, :, lanes] + low * own + high * following
            block.append(jnp.where(is_head, head, body))
        fine, quads = local_pass(block, lambda r: kappa_ref[r], first_beta, total)
        for r in range(1, n):
            next_ref[r, :, lanes] = fine[r - 1]
        for q, quad in enumerate(quads):
            packet_ref[pl.ds(q * tiles + t, na, stride=rows), :] = quad


def last_kernel(count, answer_ref, fine_ref, out_ref):
    n, na, cols = fine_ref.shape
    tiles = cols // LANES
    total = n * count
    first_beta = lax.axis_index("lvl").astype(jnp.float32) * (DRIFT / count)
    for t in range(tiles):
        lanes = slice(t * LANES, (t + 1) * LANES)
        own, following, head = (
            answer_ref[pl.ds(q * tiles + t, na, stride=3 * tiles), :] for q in range(3)
        )
        out_ref[0, :, lanes] = head
        for r in range(1, n):
            low, high = end_weights(r, n, first_beta, total)
            out_ref[r, :, lanes] = fine_ref[r, :, lanes] + low * own + high * following


def whole(count):
    return [pl.BlockSpec(memory_space=pltpu.VMEM)] * count


def call(body, name, inputs, outs, scratch=()):
    return pl.pallas_call(
        body,
        name=name,
        out_shape=[jax.ShapeDtypeStruct(shape, jnp.float32) for shape in outs],
        in_specs=whole(len(inputs)),
        out_specs=whole(len(outs)),
        scratch_shapes=[pltpu.VMEM(shape, jnp.float32) for shape in scratch],
        compiler_params=pltpu.CompilerParams(vmem_limit_bytes=VMEM_LIMIT),
    )(*inputs)


def swap(packets, axis, count):
    apart = packets.reshape(count, packets.shape[0] // count, 1, LANES)
    return lax.all_to_all(apart, axis, 0, 0).reshape(packets.shape)


def per_device(coefficients, local_vol):
    nb, na, cols = coefficients.shape
    fibs, lvls = lax.axis_size("fib"), lax.axis_size("lvl")
    tiles = cols // LANES
    per = tiles * nb // fibs
    packets, fine = call(
        functools.partial(first_kernel, fibs),
        "first",
        (coefficients, local_vol),
        ((fibs * (4 * per + 1), LANES), (nb, na, cols)),
        ((na, nb, LANES),),
    )
    packets = swap(packets, "fib", fibs)
    (answers,) = call(
        functools.partial(coarse_kernel, fibs, na, per), "coarse_a", (packets,), ((fibs * 3 * per, LANES),)
    )
    answers = swap(answers, "fib", fibs)
    packets, fine = call(
        functools.partial(second_kernel, fibs, lvls),
        "second",
        (answers, fine, local_vol),
        ((lvls * (4 * tiles + 1), LANES), (nb, na, cols)),
        ((nb, na, LANES),),
    )
    packets = swap(packets, "lvl", lvls)
    (answers,) = call(
        functools.partial(coarse_kernel, lvls, nb, tiles), "coarse_b", (packets,), ((lvls * 3 * tiles, LANES),)
    )
    answers = swap(answers, "lvl", lvls)
    (out,) = call(functools.partial(last_kernel, lvls), "last", (answers, fine), ((nb, na, cols),))
    return out


def solution(mesh):
    placed = (P("lvl", "fib", None), P("lvl", "fib"))
    return jax.shard_map(
        per_device, mesh=mesh, in_specs=placed, out_specs=P("lvl", "fib", None), check_vma=False
    )
```

```python
import functools

import jax
import jax.numpy as jnp
from jax import lax
from jax.experimental import pallas as pl
from jax.experimental.pallas import tpu as pltpu
from jax.sharding import PartitionSpec as P

KAPPA_SCALE = 8.0
DRIFT = 0.2
DISCOUNT = 0.05
CENTRE = 2.0 / 3.0 + DISCOUNT
SIDE = 1.0 / 6.0
LINEAR = CENTRE + 2.0 * SIDE
LANES = 128
CHUNKS = 4
VMEM_LIMIT = 32 * 1024 * 1024


def descend(rows, low, high):
    n = len(rows)
    nodal = [low] + [None] * (n - 1) + [high]
    step = n // 2
    while step >= 1:
        for at in range(step, n, 2 * step):
            left, right = nodal[at - step], nodal[at + step]
            if left is None and right is None:
                nodal[at] = rows[at]
            elif left is None or right is None:
                nodal[at] = rows[at] + 0.5 * (right if left is None else left)
            else:
                nodal[at] = rows[at] + 0.5 * (left + right)
        step //= 2
    return nodal


def add(a, b):
    if a is None:
        return b
    return a if b is None else a + b


def ascend(rows):
    n = len(rows)
    sums = list(rows) + [None]
    step = 1
    while step < n:
        for at in range(step, n, 2 * step):
            half = 0.5 * sums[at]
            sums[at - step] = add(sums[at - step], half)
            sums[at + step] = add(sums[at + step], half)
        step *= 2
    return sums


def lowest(index):
    return index & -index


def local_pass(rows, kappas, first_beta, total):
    n = len(rows)
    nodal = descend(rows, None, None)
    images = []
    for at in range(n):
        beta = first_beta + DRIFT * at / total
        kappa = kappas(at)
        above = nodal[at + 1]
        if at == 0:
            images.append((SIDE - beta - kappa) * above)
            continue
        below = nodal[at - 1]
        middle = nodal[at]
        image = (CENTRE + 2.0 * kappa) * middle
        if below is not None:
            image = image + (SIDE + beta - kappa) * below
        if above is not None:
            image = image + (SIDE - beta - kappa) * above
        images.append(image)
    sums = ascend(images)
    fine = [sums[at] * (1.0 / lowest(at)) for at in range(1, n)]
    return fine, (rows[0], sums[0], sums[n], nodal[n - 1])


def end_weights(at, n, first_beta, total):
    tilt = (first_beta + DRIFT * at / total) * (2.0 / n)
    return LINEAR * (1.0 - at / n) + tilt, LINEAR * (at / n) - tilt


def coarse_pass(heads, lefts, rights, lasts, kappas, n):
    count = len(heads)
    total = n * count
    inner = descend([None] + heads[1:], heads[0], None)
    node = inner[:count]
    share = [r / n for r in range(n)]
    left0 = sum(1 - s for s in share[1:])
    left1 = sum((1 - s) ** 2 for s in share[1:])
    left2 = sum((1 - s) * s for s in share[1:])
    left3 = sum((1 - s) * s * n for s in share[1:])
    right0 = sum(share[1:])
    right1 = left2
    right2 = sum(s * s for s in share[1:])
    right3 = sum(s * s * n for s in share[1:])
    slope = DRIFT / total
    duals = []
    for i in range(count):
        beta = DRIFT * i / count
        kappa = kappas[i]
        tilt = (2.0 / n) * (beta * left0 + slope * left3)
        following = node[i + 1] if i + 1 < count else None
        upper = SIDE - beta - kappa
        own = CENTRE + 2.0 * kappa + upper * (1.0 - 1.0 / n) + (LINEAR * left1 + tilt)
        dual = lefts[i]
        if following is not None:
            dual = dual + (upper * (1.0 / n) + (LINEAR * left2 - tilt)) * following
        if i > 0:
            before_beta = DRIFT * (i - 1) / count
            tilt = (2.0 / n) * (before_beta * right0 + slope * right3)
            lower = SIDE + beta - kappa
            own = own + lower * (1.0 - 1.0 / n) + (LINEAR * right2 - tilt)
            dual = dual + rights[i - 1] + lower * lasts[i - 1]
            dual = dual + (lower * (1.0 / n) + (LINEAR * right1 + tilt)) * node[i - 1]
        duals.append(dual + own * node[i])
    sums = ascend(duals)
    outs = [sums[i] * (1.0 / (total if i == 0 else n * lowest(i))) for i in range(count)]
    return node, outs


def first_kernel(count, values_ref, vol_ref, packet_ref, fine_ref, kappa_ref, stage_ref, own_vol_ref, sems):
    nb, n, cols = values_ref.shape
    tiles = cols // LANES
    total = n * count
    chunks, _, _, width = stage_ref.shape
    vol_copy = pltpu.make_async_copy(vol_ref, own_vol_ref, sems.at[chunks])
    vol_copy.start()
    copies = []
    for chunk in range(chunks):
        copies.append(
            pltpu.make_async_copy(
                values_ref.at[:, :, pl.ds(chunk * width, width)], stage_ref.at[chunk], sems.at[chunk]
            )
        )
        copies[-1].start()
    index = lax.axis_index("fib").astype(jnp.float32)
    first_beta = index * (DRIFT / count)
    vol_copy.wait()
    vol = own_vol_ref[...]
    for r in range(n):
        place = index * (1.0 / count) + r / total
        root = vol[:, r : r + 1] * place
        kappa_ref[r] = jnp.broadcast_to((KAPPA_SCALE * 0.5) * root * root, (nb, LANES))
    parts = count // nb
    per = tiles // parts
    rows = 4 * per + 1
    stride = parts * rows
    for part in range(parts):
        packet_ref[pl.ds(part * rows + rows - 1, nb, stride=stride), :] = kappa_ref[0]
    for t in range(tiles):
        copies[t].wait()
        tile = stage_ref.at[t].reshape(nb * n, LANES)
        block = [tile[pl.ds(r, nb, stride=n), :] for r in range(n)]
        fine, quads = local_pass(block, lambda r: kappa_ref[r], first_beta, total)
        fine_ref[t, pl.ds(0, nb, stride=n), :] = jnp.zeros_like(fine[0])
        for r in range(1, n):
            fine_ref[t, pl.ds(r, nb, stride=n), :] = fine[r - 1]
        for q, quad in enumerate(quads):
            start = (t // per) * rows + q * per + t % per
            packet_ref[pl.ds(start, nb, stride=stride), :] = quad


def coarse_kernel(count, n, per, packet_ref, answer_ref):
    rows = 4 * per + 1

    def piece(i, q):
        return packet_ref[i * rows + q * per : i * rows + (q + 1) * per, :]

    quads = [[piece(i, q) for i in range(count)] for q in range(4)]
    kappas = [packet_ref[(i + 1) * rows - 1 : (i + 1) * rows, :] for i in range(count)]
    node, outs = coarse_pass(*quads, kappas, n)
    for i in range(count):
        base = 3 * per * i
        answer_ref[base : base + per, :] = node[i]
        answer_ref[base + per : base + 2 * per, :] = (
            node[i + 1] if i + 1 < count else jnp.zeros_like(node[i])
        )
        answer_ref[base + 2 * per : base + 3 * per, :] = outs[i]


def second_kernel(fib_count, lvl_count, answer_ref, fine_ref, vol_ref, packet_ref, next_ref, kappa_ref):
    n, na, _ = next_ref.shape
    tiles = fine_ref.shape[0]
    fib_total = na * fib_count
    total = n * lvl_count
    fib_beta = lax.axis_index("fib").astype(jnp.float32) * (DRIFT / fib_count)
    index = lax.axis_index("lvl").astype(jnp.float32)
    first_beta = index * (DRIFT / lvl_count)
    vol = vol_ref[...]
    diagonal = lax.broadcasted_iota(jnp.int32, (na, na), 0) == lax.broadcasted_iota(
        jnp.int32, (na, na), 1
    )
    for r in range(n):
        place = index * (1.0 / lvl_count) + r / total
        column = jnp.sum(jnp.where(diagonal, vol[r : r + 1, :], 0.0), axis=1, keepdims=True)
        root = column * place
        kappa_ref[r] = jnp.broadcast_to((KAPPA_SCALE * 0.5) * root * root, (na, LANES))
    at = lax.broadcasted_iota(jnp.int32, (na, LANES), 0)
    tilt = (fib_beta + at.astype(jnp.float32) * (DRIFT / fib_total)) * (2.0 / na)
    share = at.astype(jnp.float32) * (1.0 / na)
    is_head = at == 0
    low = LINEAR * (1.0 - share) + tilt
    high = LINEAR * share - tilt
    parts = fib_count // n
    per = tiles // parts
    rows = 4 * tiles + 1
    packet_ref[pl.ds(rows - 1, na, stride=rows), :] = kappa_ref[0]
    for t in range(tiles):
        lanes = slice(t * LANES, (t + 1) * LANES)
        block = []
        for b in range(n):
            base = (b * parts + t // per) * 3 * per + t % per
            own = answer_ref[base : base + 1, :]
            following = answer_ref[base + per : base + per + 1, :]
            head = answer_ref[base + 2 * per : base + 2 * per + 1, :]
            body = fine_ref[t, b * na : (b + 1) * na, :] + low * own + high * following
            block.append(jnp.where(is_head, head, body))
        fine, quads = local_pass(block, lambda r: kappa_ref[r], first_beta, total)
        for r in range(1, n):
            next_ref[r, :, lanes] = fine[r - 1]
        for q, quad in enumerate(quads):
            packet_ref[pl.ds(q * tiles + t, na, stride=rows), :] = quad


def last_kernel(count, answer_ref, fine_ref, out_ref, stage_ref, sems):
    n, na, cols = fine_ref.shape
    tiles = cols // LANES
    total = n * count
    first_beta = lax.axis_index("lvl").astype(jnp.float32) * (DRIFT / count)
    chunks, deep = stage_ref.shape[:2]
    copies = []
    for chunk in range(chunks):
        for t in range(tiles):
            lanes = slice(t * LANES, (t + 1) * LANES)
            own, following, head = (
                answer_ref[pl.ds(q * tiles + t, na, stride=3 * tiles), :] for q in range(3)
            )
            for at in range(deep):
                r = chunk * deep + at
                if r == 0:
                    stage_ref[chunk, at, :, lanes] = head
                    continue
                low, high = end_weights(r, n, first_beta, total)
                stage_ref[chunk, at, :, lanes] = fine_ref[r, :, lanes] + low * own + high * following
        copies.append(
            pltpu.make_async_copy(
                stage_ref.at[chunk], out_ref.at[pl.ds(chunk * deep, deep)], sems.at[chunk]
            )
        )
        copies[-1].start()
    for copy in copies:
        copy.wait()


def call(body, name, inputs, outs, scratch=(), copies=0, far_in=(), far_out=()):
    near, far = pl.BlockSpec(memory_space=pltpu.VMEM), pl.BlockSpec(memory_space=pltpu.HBM)
    rooms = [pltpu.VMEM(shape, jnp.float32) for shape in scratch]
    if copies:
        rooms.append(pltpu.SemaphoreType.DMA((copies,)))
    return pl.pallas_call(
        body,
        name=name,
        out_shape=[jax.ShapeDtypeStruct(shape, jnp.float32) for shape in outs],
        in_specs=[far if i in far_in else near for i in range(len(inputs))],
        out_specs=[far if i in far_out else near for i in range(len(outs))],
        scratch_shapes=rooms,
        compiler_params=pltpu.CompilerParams(vmem_limit_bytes=VMEM_LIMIT),
    )(*(pltpu.with_memory_space_constraint(x, pltpu.HBM) if i in far_in else x for i, x in enumerate(inputs)))


def swap(packets, axis, count):
    apart = packets.reshape(count, packets.shape[0] // count, 1, LANES)
    return lax.all_to_all(apart, axis, 0, 0).reshape(packets.shape)


def per_device(coefficients, local_vol):
    nb, na, cols = coefficients.shape
    fibs, lvls = lax.axis_size("fib"), lax.axis_size("lvl")
    tiles = cols // LANES
    per = tiles * nb // fibs
    packets, fine = call(
        functools.partial(first_kernel, fibs),
        "first",
        (coefficients, local_vol),
        ((fibs * (4 * per + 1), LANES), (tiles, nb * na, LANES)),
        ((na, nb, LANES), (tiles, nb, na, LANES), (nb, na)),
        copies=tiles + 1,
        far_in=(0, 1),
    )
    packets = swap(packets, "fib", fibs)
    (answers,) = call(
        functools.partial(coarse_kernel, fibs, na, per), "coarse_a", (packets,), ((fibs * 3 * per, LANES),)
    )
    answers = swap(answers, "fib", fibs)
    packets, fine = call(
        functools.partial(second_kernel, fibs, lvls),
        "second",
        (answers, fine, local_vol),
        ((lvls * (4 * tiles + 1), LANES), (nb, na, cols)),
        ((nb, na, LANES),),
    )
    packets = swap(packets, "lvl", lvls)
    (answers,) = call(
        functools.partial(coarse_kernel, lvls, nb, tiles), "coarse_b", (packets,), ((lvls * 3 * tiles, LANES),)
    )
    answers = swap(answers, "lvl", lvls)
    (out,) = call(
        functools.partial(last_kernel, lvls),
        "last",
        (answers, fine),
        ((nb, na, cols),),
        ((CHUNKS, nb // CHUNKS, na, cols),),
        copies=CHUNKS,
        far_out=(0,),
    )
    return out


def solution(mesh):
    placed = (P("lvl", "fib", None), P("lvl", "fib"))
    return jax.shard_map(
        per_device, mesh=mesh, in_specs=placed, out_specs=P("lvl", "fib", None), check_vma=False
    )
```

```python
import functools

import jax
import jax.numpy as jnp
from jax import lax
from jax.experimental import pallas as pl
from jax.experimental.pallas import tpu as pltpu
from jax.sharding import PartitionSpec as P

KAPPA_SCALE = 8.0
DRIFT = 0.2
DISCOUNT = 0.05
CENTRE = 2.0 / 3.0 + DISCOUNT
SIDE = 1.0 / 6.0
LINEAR = CENTRE + 2.0 * SIDE
LANES = 128
CHUNKS = 4
VMEM_LIMIT = 32 * 1024 * 1024


def descend(rows, low, high):
    n = len(rows)
    nodal = [low] + [None] * (n - 1) + [high]
    step = n // 2
    while step >= 1:
        for at in range(step, n, 2 * step):
            left, right = nodal[at - step], nodal[at + step]
            if left is None and right is None:
                nodal[at] = rows[at]
            elif left is None or right is None:
                nodal[at] = rows[at] + 0.5 * (right if left is None else left)
            else:
                nodal[at] = rows[at] + 0.5 * (left + right)
        step //= 2
    return nodal


def add(a, b):
    if a is None:
        return b
    return a if b is None else a + b


def ascend(rows):
    n = len(rows)
    sums = list(rows) + [None]
    step = 1
    while step < n:
        for at in range(step, n, 2 * step):
            half = 0.5 * sums[at]
            sums[at - step] = add(sums[at - step], half)
            sums[at + step] = add(sums[at + step], half)
        step *= 2
    return sums


def lowest(index):
    return index & -index


def local_pass(rows, kappas, first_beta, total):
    n = len(rows)
    nodal = descend(rows, None, None)
    images = []
    for at in range(n):
        beta = first_beta + DRIFT * at / total
        kappa = kappas(at)
        above = nodal[at + 1]
        if at == 0:
            images.append((SIDE - beta - kappa) * above)
            continue
        below = nodal[at - 1]
        middle = nodal[at]
        image = (CENTRE + 2.0 * kappa) * middle
        if below is not None:
            image = image + (SIDE + beta - kappa) * below
        if above is not None:
            image = image + (SIDE - beta - kappa) * above
        images.append(image)
    sums = ascend(images)
    fine = [sums[at] * (1.0 / lowest(at)) for at in range(1, n)]
    return fine, (rows[0], sums[0], sums[n], nodal[n - 1])


def end_weights(at, n, first_beta, total):
    tilt = (first_beta + DRIFT * at / total) * (2.0 / n)
    return LINEAR * (1.0 - at / n) + tilt, LINEAR * (at / n) - tilt


def coarse_pass(heads, lefts, rights, lasts, kappas, n):
    count = len(heads)
    total = n * count
    inner = descend([None] + heads[1:], heads[0], None)
    node = inner[:count]
    share = [r / n for r in range(n)]
    left0 = sum(1 - s for s in share[1:])
    left1 = sum((1 - s) ** 2 for s in share[1:])
    left2 = sum((1 - s) * s for s in share[1:])
    left3 = sum((1 - s) * s * n for s in share[1:])
    right0 = sum(share[1:])
    right1 = left2
    right2 = sum(s * s for s in share[1:])
    right3 = sum(s * s * n for s in share[1:])
    slope = DRIFT / total
    duals = []
    for i in range(count):
        beta = DRIFT * i / count
        kappa = kappas[i]
        tilt = (2.0 / n) * (beta * left0 + slope * left3)
        following = node[i + 1] if i + 1 < count else None
        upper = SIDE - beta - kappa
        own = CENTRE + 2.0 * kappa + upper * (1.0 - 1.0 / n) + (LINEAR * left1 + tilt)
        dual = lefts[i]
        if following is not None:
            dual = dual + (upper * (1.0 / n) + (LINEAR * left2 - tilt)) * following
        if i > 0:
            before_beta = DRIFT * (i - 1) / count
            tilt = (2.0 / n) * (before_beta * right0 + slope * right3)
            lower = SIDE + beta - kappa
            own = own + lower * (1.0 - 1.0 / n) + (LINEAR * right2 - tilt)
            dual = dual + rights[i - 1]
            if lasts is not None:
                dual = dual + lower * lasts[i - 1]
            dual = dual + (lower * (1.0 / n) + (LINEAR * right1 + tilt)) * node[i - 1]
        duals.append(dual + own * node[i])
    sums = ascend(duals)
    outs = [sums[i] * (1.0 / (total if i == 0 else n * lowest(i))) for i in range(count)]
    return node, outs


def first_kernel(count, values_ref, vol_ref, packet_ref, fine_ref, kappa_ref, stage_ref, own_vol_ref, sems):
    nb, n, cols = values_ref.shape
    tiles = cols // LANES
    total = n * count
    chunks, _, _, width = stage_ref.shape
    vol_copy = pltpu.make_async_copy(vol_ref, own_vol_ref, sems.at[chunks])
    vol_copy.start()
    copies = []
    for chunk in range(chunks):
        copies.append(
            pltpu.make_async_copy(
                values_ref.at[:, :, pl.ds(chunk * width, width)], stage_ref.at[chunk], sems.at[chunk]
            )
        )
        copies[-1].start()
    index = lax.axis_index("fib").astype(jnp.float32)
    first_beta = index * (DRIFT / count)
    vol_copy.wait()
    vol = own_vol_ref[...]
    for r in range(n):
        place = index * (1.0 / count) + r / total
        root = vol[:, r : r + 1] * place
        kappa_ref[r] = jnp.broadcast_to((KAPPA_SCALE * 0.5) * root * root, (nb, LANES))
    parts = count // nb
    per = tiles // parts
    rows = 4 * per + 1
    stride = parts * rows
    for part in range(parts):
        packet_ref[pl.ds(part * rows + rows - 1, nb, stride=stride), :] = kappa_ref[0]
    for t in range(tiles):
        copies[t].wait()
        tile = stage_ref.at[t].reshape(nb * n, LANES)
        block = [tile[pl.ds(r, nb, stride=n), :] for r in range(n)]
        fine, quads = local_pass(block, lambda r: kappa_ref[r], first_beta, total)
        fine_ref[t, pl.ds(0, nb, stride=n), :] = jnp.zeros_like(fine[0])
        for r in range(1, n):
            fine_ref[t, pl.ds(r, nb, stride=n), :] = fine[r - 1]
        for q, quad in enumerate(quads):
            start = (t // per) * rows + q * per + t % per
            packet_ref[pl.ds(start, nb, stride=stride), :] = quad


def coarse_kernel(count, n, per, kinds, packet_ref, answer_ref):
    rows = kinds * per + 1

    def piece(i, q):
        return packet_ref[i * rows + q * per : i * rows + (q + 1) * per, :]

    quads = [[piece(i, q) for i in range(count)] if q < kinds else None for q in range(4)]
    kappas = [packet_ref[(i + 1) * rows - 1 : (i + 1) * rows, :] for i in range(count)]
    node, outs = coarse_pass(*quads, kappas, n)
    for i in range(count):
        base = 3 * per * i
        answer_ref[base : base + per, :] = node[i]
        answer_ref[base + per : base + 2 * per, :] = (
            node[i + 1] if i + 1 < count else jnp.zeros_like(node[i])
        )
        answer_ref[base + 2 * per : base + 3 * per, :] = outs[i]


def second_kernel(fib_count, lvl_count, answer_ref, fine_ref, vol_ref, next_vol_ref, packet_ref, next_ref, kappa_ref):
    n, na, _ = next_ref.shape
    tiles = fine_ref.shape[0]
    fib_total = na * fib_count
    total = n * lvl_count
    fib_beta = lax.axis_index("fib").astype(jnp.float32) * (DRIFT / fib_count)
    index = lax.axis_index("lvl").astype(jnp.float32)
    first_beta = index * (DRIFT / lvl_count)
    vol = vol_ref[...]
    diagonal = lax.broadcasted_iota(jnp.int32, (na, na), 0) == lax.broadcasted_iota(
        jnp.int32, (na, na), 1
    )
    for r in range(n + 1):
        place = index * (1.0 / lvl_count) + r / total
        row = next_vol_ref[0:1, :] if r == n else vol[r : r + 1, :]
        column = jnp.sum(jnp.where(diagonal, row, 0.0), axis=1, keepdims=True)
        root = column * place
        kappa_ref[r] = jnp.broadcast_to((KAPPA_SCALE * 0.5) * root * root, (na, LANES))
    at = lax.broadcasted_iota(jnp.int32, (na, LANES), 0)
    tilt = (fib_beta + at.astype(jnp.float32) * (DRIFT / fib_total)) * (2.0 / na)
    share = at.astype(jnp.float32) * (1.0 / na)
    is_head = at == 0
    low = LINEAR * (1.0 - share) + tilt
    high = LINEAR * share - tilt
    parts = fib_count // n
    per = tiles // parts
    rows = 3 * tiles + 1
    next_lower = SIDE + (first_beta + DRIFT / lvl_count) - kappa_ref[n]
    packet_ref[pl.ds(rows - 1, na, stride=rows), :] = kappa_ref[0]
    for t in range(tiles):
        lanes = slice(t * LANES, (t + 1) * LANES)
        block = []
        for b in range(n):
            base = (b * parts + t // per) * 3 * per + t % per
            own = answer_ref[base : base + 1, :]
            following = answer_ref[base + per : base + per + 1, :]
            head = answer_ref[base + 2 * per : base + 2 * per + 1, :]
            body = fine_ref[t, b * na : (b + 1) * na, :] + low * own + high * following
            block.append(jnp.where(is_head, head, body))
        fine, (first, left, right, final) = local_pass(block, lambda r: kappa_ref[r], first_beta, total)
        for r in range(1, n):
            next_ref[r, :, lanes] = fine[r - 1]
        for q, row in enumerate((first, left, right + next_lower * final)):
            packet_ref[pl.ds(q * tiles + t, na, stride=rows), :] = row


def last_kernel(count, answer_ref, fine_ref, out_ref, stage_ref, sems):
    n, na, cols = fine_ref.shape
    tiles = cols // LANES
    total = n * count
    first_beta = lax.axis_index("lvl").astype(jnp.float32) * (DRIFT / count)
    chunks, deep = stage_ref.shape[:2]
    copies = []
    for chunk in range(chunks):
        for t in range(tiles):
            lanes = slice(t * LANES, (t + 1) * LANES)
            own, following, head = (
                answer_ref[pl.ds(q * tiles + t, na, stride=3 * tiles), :] for q in range(3)
            )
            for at in range(deep):
                r = chunk * deep + at
                if r == 0:
                    stage_ref[chunk, at, :, lanes] = head
                    continue
                low, high = end_weights(r, n, first_beta, total)
                stage_ref[chunk, at, :, lanes] = fine_ref[r, :, lanes] + low * own + high * following
        copies.append(
            pltpu.make_async_copy(
                stage_ref.at[chunk], out_ref.at[pl.ds(chunk * deep, deep)], sems.at[chunk]
            )
        )
        copies[-1].start()
    for copy in copies:
        copy.wait()


def call(body, name, inputs, outs, scratch=(), copies=0, far_in=(), far_out=()):
    near, far = pl.BlockSpec(memory_space=pltpu.VMEM), pl.BlockSpec(memory_space=pltpu.HBM)
    rooms = [pltpu.VMEM(shape, jnp.float32) for shape in scratch]
    if copies:
        rooms.append(pltpu.SemaphoreType.DMA((copies,)))
    return pl.pallas_call(
        body,
        name=name,
        out_shape=[jax.ShapeDtypeStruct(shape, jnp.float32) for shape in outs],
        in_specs=[far if i in far_in else near for i in range(len(inputs))],
        out_specs=[far if i in far_out else near for i in range(len(outs))],
        scratch_shapes=rooms,
        compiler_params=pltpu.CompilerParams(vmem_limit_bytes=VMEM_LIMIT),
    )(*(pltpu.with_memory_space_constraint(x, pltpu.HBM) if i in far_in else x for i, x in enumerate(inputs)))


def swap(packets, axis, count):
    apart = packets.reshape(count, packets.shape[0] // count, 1, LANES)
    return lax.all_to_all(apart, axis, 0, 0).reshape(packets.shape)


def per_device(coefficients, local_vol):
    nb, na, cols = coefficients.shape
    fibs, lvls = lax.axis_size("fib"), lax.axis_size("lvl")
    tiles = cols // LANES
    per = tiles * nb // fibs
    next_vol = lax.ppermute(local_vol, "lvl", [(i + 1, i) for i in range(lvls - 1)])
    packets, fine = call(
        functools.partial(first_kernel, fibs),
        "first",
        (coefficients, local_vol),
        ((fibs * (4 * per + 1), LANES), (tiles, nb * na, LANES)),
        ((na, nb, LANES), (tiles, nb, na, LANES), (nb, na)),
        copies=tiles + 1,
        far_in=(0, 1),
    )
    packets = swap(packets, "fib", fibs)
    (answers,) = call(
        functools.partial(coarse_kernel, fibs, na, per, 4), "coarse_a", (packets,), ((fibs * 3 * per, LANES),)
    )
    answers = swap(answers, "fib", fibs)
    packets, fine = call(
        functools.partial(second_kernel, fibs, lvls),
        "second",
        (answers, fine, local_vol, next_vol),
        ((lvls * (3 * tiles + 1), LANES), (nb, na, cols)),
        ((nb + 1, na, LANES),),
    )
    packets = swap(packets, "lvl", lvls)
    (answers,) = call(
        functools.partial(coarse_kernel, lvls, nb, tiles, 3), "coarse_b", (packets,), ((lvls * 3 * tiles, LANES),)
    )
    answers = swap(answers, "lvl", lvls)
    (out,) = call(
        functools.partial(last_kernel, lvls),
        "last",
        (answers, fine),
        ((nb, na, cols),),
        ((CHUNKS, nb // CHUNKS, na, cols),),
        copies=CHUNKS,
        far_out=(0,),
    )
    return out


def solution(mesh):
    placed = (P("lvl", "fib", None), P("lvl", "fib"))
    return jax.shard_map(
        per_device, mesh=mesh, in_specs=placed, out_specs=P("lvl", "fib", None), check_vma=False
    )
```

```python
import functools

import jax
import jax.numpy as jnp
from jax import lax
from jax.experimental import pallas as pl
from jax.experimental.pallas import tpu as pltpu
from jax.sharding import PartitionSpec as P

KAPPA_SCALE = 8.0
DRIFT = 0.2
DISCOUNT = 0.05
CENTRE = 2.0 / 3.0 + DISCOUNT
SIDE = 1.0 / 6.0
LINEAR = CENTRE + 2.0 * SIDE
LANES = 128
CHUNKS = 4
VMEM_LIMIT = 32 * 1024 * 1024


def descend(rows, low, high):
    n = len(rows)
    nodal = [low] + [None] * (n - 1) + [high]
    step = n // 2
    while step >= 1:
        for at in range(step, n, 2 * step):
            left, right = nodal[at - step], nodal[at + step]
            if left is None and right is None:
                nodal[at] = rows[at]
            elif left is None or right is None:
                nodal[at] = rows[at] + 0.5 * (right if left is None else left)
            else:
                nodal[at] = rows[at] + 0.5 * (left + right)
        step //= 2
    return nodal


def add(a, b):
    if a is None:
        return b
    return a if b is None else a + b


def ascend(rows):
    n = len(rows)
    sums = list(rows) + [None]
    step = 1
    while step < n:
        for at in range(step, n, 2 * step):
            half = 0.5 * sums[at]
            sums[at - step] = add(sums[at - step], half)
            sums[at + step] = add(sums[at + step], half)
        step *= 2
    return sums


def lowest(index):
    return index & -index


def local_pass(rows, kappas, first_beta, total):
    n = len(rows)
    nodal = descend(rows, None, None)
    images = []
    for at in range(n):
        beta = first_beta + DRIFT * at / total
        kappa = kappas(at)
        above = nodal[at + 1]
        if at == 0:
            images.append((SIDE - beta - kappa) * above)
            continue
        below = nodal[at - 1]
        middle = nodal[at]
        image = (CENTRE + 2.0 * kappa) * middle
        if below is not None:
            image = image + (SIDE + beta - kappa) * below
        if above is not None:
            image = image + (SIDE - beta - kappa) * above
        images.append(image)
    sums = ascend(images)
    fine = [sums[at] * (1.0 / lowest(at)) for at in range(1, n)]
    return fine, (rows[0], sums[0], sums[n], nodal[n - 1])


def end_weights(at, n, first_beta, total):
    tilt = (first_beta + DRIFT * at / total) * (2.0 / n)
    return LINEAR * (1.0 - at / n) + tilt, LINEAR * (at / n) - tilt


def coarse_pass(heads, lefts, rights, lasts, kappas, n):
    count = len(heads)
    total = n * count
    inner = descend([None] + heads[1:], heads[0], None)
    node = inner[:count]
    share = [r / n for r in range(n)]
    left0 = sum(1 - s for s in share[1:])
    left1 = sum((1 - s) ** 2 for s in share[1:])
    left2 = sum((1 - s) * s for s in share[1:])
    left3 = sum((1 - s) * s * n for s in share[1:])
    right0 = sum(share[1:])
    right1 = left2
    right2 = sum(s * s for s in share[1:])
    right3 = sum(s * s * n for s in share[1:])
    slope = DRIFT / total
    duals = []
    for i in range(count):
        beta = DRIFT * i / count
        kappa = kappas[i]
        tilt = (2.0 / n) * (beta * left0 + slope * left3)
        following = node[i + 1] if i + 1 < count else None
        upper = SIDE - beta - kappa
        own = CENTRE + 2.0 * kappa + upper * (1.0 - 1.0 / n) + (LINEAR * left1 + tilt)
        dual = lefts[i]
        if following is not None:
            dual = dual + (upper * (1.0 / n) + (LINEAR * left2 - tilt)) * following
        if i > 0:
            before_beta = DRIFT * (i - 1) / count
            tilt = (2.0 / n) * (before_beta * right0 + slope * right3)
            lower = SIDE + beta - kappa
            own = own + lower * (1.0 - 1.0 / n) + (LINEAR * right2 - tilt)
            dual = dual + rights[i - 1] + lower * lasts[i - 1]
            dual = dual + (lower * (1.0 / n) + (LINEAR * right1 + tilt)) * node[i - 1]
        duals.append(dual + own * node[i])
    sums = ascend(duals)
    outs = [sums[i] * (1.0 / (total if i == 0 else n * lowest(i))) for i in range(count)]
    return node, outs


def first_kernel(count, values_ref, vol_ref, packet_ref, fine_ref, kappa_ref, stage_ref, own_vol_ref, sems):
    nb, n, cols = values_ref.shape
    tiles = cols // LANES
    total = n * count
    chunks, _, _, width = stage_ref.shape
    vol_copy = pltpu.make_async_copy(vol_ref, own_vol_ref, sems.at[chunks])
    vol_copy.start()
    copies = []
    for chunk in range(chunks):
        copies.append(
            pltpu.make_async_copy(
                values_ref.at[:, :, pl.ds(chunk * width, width)], stage_ref.at[chunk], sems.at[chunk]
            )
        )
        copies[-1].start()
    index = lax.axis_index("fib").astype(jnp.float32)
    first_beta = index * (DRIFT / count)
    vol_copy.wait()
    vol = own_vol_ref[...]
    for r in range(n):
        place = index * (1.0 / count) + r / total
        root = vol[:, r : r + 1] * place
        kappa_ref[r] = jnp.broadcast_to((KAPPA_SCALE * 0.5) * root * root, (nb, LANES))
    parts = count // nb
    per = tiles // parts
    rows = 4 * per + 1
    stride = parts * rows
    for part in range(parts):
        packet_ref[pl.ds(part * rows + rows - 1, nb, stride=stride), :] = kappa_ref[0]
    for t in range(tiles):
        copies[t].wait()
        turned = jnp.swapaxes(stage_ref[t], 0, 1)
        block = [turned[r] for r in range(n)]
        fine, quads = local_pass(block, lambda r: kappa_ref[r], first_beta, total)
        fine_ref[t, pl.ds(0, nb, stride=n), :] = jnp.zeros_like(fine[0])
        for r in range(1, n):
            fine_ref[t, pl.ds(r, nb, stride=n), :] = fine[r - 1]
        for q, quad in enumerate(quads):
            start = (t // per) * rows + q * per + t % per
            packet_ref[pl.ds(start, nb, stride=stride), :] = quad


def coarse_kernel(count, n, per, packet_ref, answer_ref):
    rows = 4 * per + 1

    def piece(i, q):
        return packet_ref[i * rows + q * per : i * rows + (q + 1) * per, :]

    quads = [[piece(i, q) for i in range(count)] for q in range(4)]
    kappas = [packet_ref[(i + 1) * rows - 1 : (i + 1) * rows, :] for i in range(count)]
    node, outs = coarse_pass(*quads, kappas, n)
    for i in range(count):
        base = 3 * per * i
        answer_ref[base : base + per, :] = node[i]
        answer_ref[base + per : base + 2 * per, :] = (
            node[i + 1] if i + 1 < count else jnp.zeros_like(node[i])
        )
        answer_ref[base + 2 * per : base + 3 * per, :] = outs[i]


def second_kernel(fib_count, lvl_count, answer_ref, fine_ref, vol_ref, packet_ref, next_ref, kappa_ref):
    n, na, _ = next_ref.shape
    tiles = fine_ref.shape[0]
    fib_total = na * fib_count
    total = n * lvl_count
    fib_beta = lax.axis_index("fib").astype(jnp.float32) * (DRIFT / fib_count)
    index = lax.axis_index("lvl").astype(jnp.float32)
    first_beta = index * (DRIFT / lvl_count)
    vol = vol_ref[...]
    diagonal = lax.broadcasted_iota(jnp.int32, (na, na), 0) == lax.broadcasted_iota(
        jnp.int32, (na, na), 1
    )
    for r in range(n):
        place = index * (1.0 / lvl_count) + r / total
        column = jnp.sum(jnp.where(diagonal, vol[r : r + 1, :], 0.0), axis=1, keepdims=True)
        root = column * place
        kappa_ref[r] = jnp.broadcast_to((KAPPA_SCALE * 0.5) * root * root, (na, LANES))
    at = lax.broadcasted_iota(jnp.int32, (na, LANES), 0)
    tilt = (fib_beta + at.astype(jnp.float32) * (DRIFT / fib_total)) * (2.0 / na)
    share = at.astype(jnp.float32) * (1.0 / na)
    is_head = at == 0
    low = LINEAR * (1.0 - share) + tilt
    high = LINEAR * share - tilt
    parts = fib_count // n
    per = tiles // parts
    rows = 4 * tiles + 1
    packet_ref[pl.ds(rows - 1, na, stride=rows), :] = kappa_ref[0]
    for t in range(tiles):
        lanes = slice(t * LANES, (t + 1) * LANES)
        block = []
        for b in range(n):
            base = (b * parts + t // per) * 3 * per + t % per
            own = answer_ref[base : base + 1, :]
            following = answer_ref[base + per : base + per + 1, :]
            head = answer_ref[base + 2 * per : base + 2 * per + 1, :]
            body = fine_ref[t, b * na : (b + 1) * na, :] + low * own + high * following
            block.append(jnp.where(is_head, head, body))
        fine, quads = local_pass(block, lambda r: kappa_ref[r], first_beta, total)
        for r in range(1, n):
            next_ref[r, :, lanes] = fine[r - 1]
        for q, quad in enumerate(quads):
            packet_ref[pl.ds(q * tiles + t, na, stride=rows), :] = quad


def last_kernel(count, answer_ref, fine_ref, out_ref, stage_ref, sems):
    n, na, cols = fine_ref.shape
    tiles = cols // LANES
    total = n * count
    first_beta = lax.axis_index("lvl").astype(jnp.float32) * (DRIFT / count)
    chunks, deep = stage_ref.shape[:2]
    copies = []
    for chunk in range(chunks):
        for t in range(tiles):
            lanes = slice(t * LANES, (t + 1) * LANES)
            own, following, head = (
                answer_ref[pl.ds(q * tiles + t, na, stride=3 * tiles), :] for q in range(3)
            )
            for at in range(deep):
                r = chunk * deep + at
                if r == 0:
                    stage_ref[chunk, at, :, lanes] = head
                    continue
                low, high = end_weights(r, n, first_beta, total)
                stage_ref[chunk, at, :, lanes] = fine_ref[r, :, lanes] + low * own + high * following
        copies.append(
            pltpu.make_async_copy(
                stage_ref.at[chunk], out_ref.at[pl.ds(chunk * deep, deep)], sems.at[chunk]
            )
        )
        copies[-1].start()
    for copy in copies:
        copy.wait()


def call(body, name, inputs, outs, scratch=(), copies=0, far_in=(), far_out=()):
    near, far = pl.BlockSpec(memory_space=pltpu.VMEM), pl.BlockSpec(memory_space=pltpu.HBM)
    rooms = [pltpu.VMEM(shape, jnp.float32) for shape in scratch]
    if copies:
        rooms.append(pltpu.SemaphoreType.DMA((copies,)))
    return pl.pallas_call(
        body,
        name=name,
        out_shape=[jax.ShapeDtypeStruct(shape, jnp.float32) for shape in outs],
        in_specs=[far if i in far_in else near for i in range(len(inputs))],
        out_specs=[far if i in far_out else near for i in range(len(outs))],
        scratch_shapes=rooms,
        compiler_params=pltpu.CompilerParams(vmem_limit_bytes=VMEM_LIMIT),
    )(*(pltpu.with_memory_space_constraint(x, pltpu.HBM) if i in far_in else x for i, x in enumerate(inputs)))


def swap(packets, axis, count):
    apart = packets.reshape(count, packets.shape[0] // count, 1, LANES)
    return lax.all_to_all(apart, axis, 0, 0).reshape(packets.shape)


def per_device(coefficients, local_vol):
    nb, na, cols = coefficients.shape
    fibs, lvls = lax.axis_size("fib"), lax.axis_size("lvl")
    tiles = cols // LANES
    per = tiles * nb // fibs
    packets, fine = call(
        functools.partial(first_kernel, fibs),
        "first",
        (coefficients, local_vol),
        ((fibs * (4 * per + 1), LANES), (tiles, nb * na, LANES)),
        ((na, nb, LANES), (tiles, nb, na, LANES), (nb, na)),
        copies=tiles + 1,
        far_in=(0, 1),
    )
    packets = swap(packets, "fib", fibs)
    (answers,) = call(
        functools.partial(coarse_kernel, fibs, na, per), "coarse_a", (packets,), ((fibs * 3 * per, LANES),)
    )
    answers = swap(answers, "fib", fibs)
    packets, fine = call(
        functools.partial(second_kernel, fibs, lvls),
        "second",
        (answers, fine, local_vol),
        ((lvls * (4 * tiles + 1), LANES), (nb, na, cols)),
        ((nb, na, LANES),),
    )
    packets = swap(packets, "lvl", lvls)
    (answers,) = call(
        functools.partial(coarse_kernel, lvls, nb, tiles), "coarse_b", (packets,), ((lvls * 3 * tiles, LANES),)
    )
    answers = swap(answers, "lvl", lvls)
    (out,) = call(
        functools.partial(last_kernel, lvls),
        "last",
        (answers, fine),
        ((nb, na, cols),),
        ((CHUNKS, nb // CHUNKS, na, cols),),
        copies=CHUNKS,
        far_out=(0,),
    )
    return out


def solution(mesh):
    placed = (P("lvl", "fib", None), P("lvl", "fib"))
    return jax.shard_map(
        per_device, mesh=mesh, in_specs=placed, out_specs=P("lvl", "fib", None), check_vma=False
    )
```
